32 devices in a mesh: row: 8 (over z, y), rep: 4 (over x, core).
Axes of the slice: x: 2, y: 2, z: 4, core: 2. Of those that a mesh axis runs over, the one named last changes fastest.
Arguments:
- feats: bfloat16 [12288, 256], P(('row', 'rep')), may hold values from -6 to 6
- weight: bfloat16 [256, 256], replicated, may hold values from -0.375 to 0.375
- bias: float32 [256], replicated, may hold values from -4 to 4
- degree: int32 [12288], P('row'), may hold values from 4 to 64
- tile_rows: int32 [8, 4, 176], P('row', 'rep'), may hold values from 0 to 11
- tile_cols: int32 [8, 4, 176], P('row', 'rep'), may hold values from 0 to 23
- tile_counts: int32 [8, 4, 176, 128, 128], P('row', 'rep'), may hold values from 0 to 3, as said below
- live_tiles: int32 [8, 4], P('row', 'rep'), may hold values from 22 to 176, as said below
- cotangent: bfloat16 [12288, 256], P(('row', 'rep')), may hold values from -6 to 6
Outputs:
- output: bfloat16 [12288, 256], P(('row', 'rep'))
- grad_feats: bfloat16 [12288, 256], P(('row', 'rep'))
- grad_weight: float32 [256, 256], replicated
- grad_bias: float32 [256], replicated
The draws below stay inside these ranges and needn't reach their ends.
Inputs may be any that keep to these rules, and one draw needn't show every extreme that they name: A device uses its first live_tiles slots; the others are not part of the adjacency. Some device has all 176 slots in use in every draw. `tile_rows`: tile positions of a device may repeat. `tile_cols`: tile positions of a device may repeat. `tile_counts`: most entries of a tile are zero.
All inputs are finite; a program needn't handle non-finite values.
Results may differ from the reference program's by a relative error of at most 0.006.
Values may be sent and summed in bfloat16 or wider, within the bound.
No kernel may reach another device: no remote copies, remote signals or barrier semaphores. Data moves between devices by JAX's collectives and lax.ppermute only.
A program may use at most 128 MiB of HBM per device.

```python
import jax
import jax.numpy as jnp
from jax import lax

F = 256
TS = 128
NODE_DEV = 384
TILES = 176
NODES = 12288
N_ROW = 8
N_REP = 4


def draw_live_tiles(key, part):
    first_key, second_key = jax.random.split(jax.random.fold_in(key, 7))
    levels = TILES // 8 * jax.random.randint(first_key, (N_ROW * N_REP,), 1, 5, dtype=jnp.int32)
    chosen = jax.random.randint(second_key, (), 0, N_ROW * N_REP, dtype=jnp.int32)
    positions = jnp.arange(N_ROW * N_REP, dtype=jnp.int32)
    flattened = jnp.where(positions == chosen, jnp.int32(TILES), levels)
    return flattened.reshape(N_ROW, N_REP)


def draw_tile_counts(key, part):
    count_key = jax.random.fold_in(key, 11)
    picks = jax.random.randint(count_key, (N_ROW, N_REP, TILES, TS, TS), 0, 3 * TS, dtype=jnp.int32)
    return jnp.where(picks < 12, picks // 4 + 1, jnp.zeros_like(picks)).astype(jnp.int32)


def plant(result, key, smallest, high):
    extent = result.shape
    index_at = [jax.random.randint(jax.random.fold_in(key, axis), (), 0, extent[axis]) for axis in range(len(extent))]
    result = result.at[tuple(index_at)].set(smallest)
    longest = extent.index(max(extent))
    index_at[longest] = (index_at[longest] + 1) % extent[longest]
    return result.at[tuple(index_at)].set(high)


def block_scale(own_key, dims, cuts, low, largest):
    gain, own = 1.0, jax.random.fold_in(own_key, 6)
    for position, parts in cuts:
        steps = jnp.exp(jax.random.uniform(jax.random.fold_in(own, position), (parts,), jnp.float32, low / len(cuts), largest / len(cuts)))
        gain = gain * jnp.repeat(steps, dims[position] // parts).reshape([-1 if axis == position else 1 for axis in range(len(dims))])
    return gain


def scatter_about(rng, dims, scale, limit, cuts=(), kind=jnp.bfloat16):
    loudness = block_scale(rng, dims, cuts, -0.22, 0.18) if cuts else 1.0
    entries = jax.random.normal(rng, dims, jnp.float32) * scale * loudness
    return jnp.minimum(jnp.maximum(entries, -limit), limit).astype(kind)


def setup_inputs(seed: int = 0) -> dict:
    splits = jax.random.split(jax.random.key(seed), 10)
    feats = scatter_about(splits[0], (NODES, F), 1.0, 6.0, ((0, 32),))
    weight = scatter_about(splits[1], (F, F), F ** -0.5, 0.375)
    bias = scatter_about(splits[2], (F,), 1.0, 4.0, (), jnp.float32)
    degree = plant(jax.random.randint(splits[3], (NODES,), 4, 65), jax.random.fold_in(splits[3], 1), 4, 64).astype(jnp.int32)
    tile_rows = plant(jax.random.randint(splits[4], (N_ROW, N_REP, TILES), 0, NODE_DEV * N_REP // TS), jax.random.fold_in(splits[4], 1), 0, (NODE_DEV * N_REP // TS) - 1).astype(jnp.int32)
    tile_cols = plant(jax.random.randint(splits[5], (N_ROW, N_REP, TILES), 0, NODE_DEV * N_ROW // TS), jax.random.fold_in(splits[5], 1), 0, (NODE_DEV * N_ROW // TS) - 1).astype(jnp.int32)
    tile_counts = draw_tile_counts(jax.random.fold_in(splits[9], 71), 0)
    live_tiles = draw_live_tiles(jax.random.fold_in(splits[9], 71), 0)
    cotangent = scatter_about(splits[8], (NODES, F), 1.0, 6.0, ((0, 32),))
    return dict(feats=feats, weight=weight, bias=bias, degree=degree, tile_rows=tile_rows, tile_cols=tile_cols, tile_counts=tile_counts, live_tiles=live_tiles, cotangent=cotangent)


def tile_products(source, chosen, counts, live, transpose):
    tile_size = counts.shape[-1]

    def one_piece(tile_index):
        return lax.dynamic_slice_in_dim(source, (tile_index * tile_size).astype(jnp.int32), tile_size, 0)
    pieces = jax.vmap(one_piece)(chosen).astype(jnp.float32)
    matrices = counts.astype(jnp.float32)
    if transpose:
        matrices = jnp.swapaxes(matrices, 1, 2)
    products = jnp.einsum('gij,gjf->gif', matrices, pieces)
    active = jnp.arange(counts.shape[0], dtype=jnp.int32) < live
    return jnp.where(active[:, None, None], products, jnp.zeros_like(products))

def reference(feats, weight, bias, degree, tile_rows, tile_cols, tile_counts, live_tiles, cotangent):
    node_count, feature_width = feats.shape
    row_nodes = NODE_DEV * N_REP
    col_nodes = NODE_DEV * N_ROW
    inv_sqrt = lax.rsqrt(degree.astype(jnp.float32))
    scaled_q = (inv_sqrt[:, None] * jnp.dot(feats, weight, preferred_element_type=jnp.float32)).astype(jnp.bfloat16)
    q_blocks = scaled_q.reshape(N_ROW, N_REP, NODE_DEV, feature_width)
    row_ids = tile_rows.reshape(-1, TILES)
    col_ids = tile_cols.reshape(-1, TILES)
    counts_all = tile_counts.reshape(-1, TILES, TS, TS)
    live_all = live_tiles.reshape(-1)
    devices = jnp.arange(N_ROW * N_REP, dtype=jnp.int32)

    def forward_step(running, device):
        row_index = device // N_REP
        column = device % N_REP
        source = lax.dynamic_index_in_dim(q_blocks, column, 1, keepdims=False).reshape(col_nodes, feature_width)
        products = tile_products(source, col_ids[device], counts_all[device], live_all[device], False)
        partial_value = jax.ops.segment_sum(products, row_ids[device], num_segments=row_nodes // TS).reshape(row_nodes, feature_width)
        current = lax.dynamic_index_in_dim(running, row_index, 0, keepdims=False)
        return (lax.dynamic_update_index_in_dim(running, current + partial_value, row_index, 0), None)
    sums, _ = lax.scan(forward_step, jnp.zeros((N_ROW, row_nodes, feature_width), jnp.float32), devices)
    aggregated = sums.reshape(node_count, feature_width)
    z_value = inv_sqrt[:, None] * (aggregated + scaled_q.astype(jnp.float32)) + bias
    sigmoid_z = jax.nn.sigmoid(z_value)
    output = (z_value * sigmoid_z).astype(jnp.bfloat16)
    grad_z = cotangent.astype(jnp.float32) * sigmoid_z * (1.0 + z_value * (1.0 - sigmoid_z))
    grad_bias = lax.optimization_barrier(jnp.sum(grad_z, axis=0))
    scaled_r = (inv_sqrt[:, None] * grad_z).astype(jnp.bfloat16)
    r_blocks = scaled_r.reshape(N_ROW, row_nodes, feature_width)

    def backward_step(running, device):
        row_index = device // N_REP
        column = device % N_REP
        source = lax.dynamic_index_in_dim(r_blocks, row_index, 0, keepdims=False)
        products = tile_products(source, row_ids[device], counts_all[device], live_all[device], True)
        partial_value = jax.ops.segment_sum(products, col_ids[device], num_segments=col_nodes // TS).reshape(col_nodes, feature_width)
        current = lax.dynamic_index_in_dim(running, column, 0, keepdims=False)
        return (lax.dynamic_update_index_in_dim(running, current + partial_value, column, 0), None)
    backward_sums, _ = lax.scan(backward_step, jnp.zeros((N_REP, col_nodes, feature_width), jnp.float32), devices)
    gathered_u = backward_sums.reshape(N_REP, N_ROW, NODE_DEV, feature_width).transpose(1, 0, 2, 3).reshape(node_count, feature_width)
    grad_q = gathered_u + scaled_r.astype(jnp.float32)
    v_full = inv_sqrt[:, None] * grad_q
    grad_weight = jnp.dot(feats.astype(jnp.float32).T, v_full, precision=lax.Precision.HIGHEST, preferred_element_type=jnp.float32)
    v_half = v_full.astype(jnp.bfloat16)
    grad_feats = jnp.dot(v_half, weight.T, preferred_element_type=jnp.float32).astype(jnp.bfloat16)
    return (output, grad_feats, grad_weight, grad_bias)
```

```python
import functools

import jax
import jax.numpy as jnp
from jax import lax
from jax.experimental import pallas as pl
from jax.experimental.pallas import tpu as pltpu
from jax.sharding import PartitionSpec as P

tiles_per_turn = 8
chunk_tiles = 16
group_tiles = 4
dense_limit = 512
tail_rows = 16
f32 = jnp.float32
bf16 = jnp.bfloat16


def swap(value, axis, distance):
    size = lax.axis_size(axis)
    return lax.ppermute(value, axis, [(i, i ^ distance) for i in range(size)])


def divide(value, divisor, limit):
    factor = (1 << 16) // divisor + 1
    assert all(n * factor >> 16 == n // divisor for n in range(limit))
    return (value * factor) >> 16


def dense_kernel(
    rows_hbm, cols_hbm, live_ref, counts_ref, acc, held, exact, rows_ref, cols_ref,
    in_sems, small_sems, *, row_tiles, col_tiles, tiles_dev
):
    slots, size, _ = held.shape
    chunk = slots // in_sems.shape[0]
    half_cols = acc.shape[1]
    half_rep = row_tiles // tiles_dev // 2
    row, rep = lax.axis_index("row"), lax.axis_index("rep")

    small_copies = [
        pltpu.make_async_copy(source, target, small_sems.at[index])
        for index, (source, target) in enumerate(
            [(rows_hbm, rows_ref), (cols_hbm, cols_ref)]
        )
    ]
    for copy in small_copies:
        copy.start()

    def chunk_copy(index):
        part = pl.ds(index * chunk, chunk)
        return pltpu.make_async_copy(counts_ref.at[part], held.at[part], in_sems.at[index])

    def start_copy(index, carry):
        chunk_copy(index).start()
        return carry

    lax.fori_loop(0, slots // chunk, start_copy, 0)

    def clear(index, carry):
        part = pl.ds(pl.multiple_of(index * size, size), size)
        acc[part] = jnp.zeros((size, half_cols), bf16)
        return carry

    lax.fori_loop(0, acc.shape[0] // size, clear, 0)
    for copy in small_copies:
        copy.wait()
    live = live_ref[0, 0]

    def place(slot):
        tile_row, tile_col = rows_ref[0, 0, slot], cols_ref[0, 0, slot]
        row_owner = divide(tile_row, tiles_dev, row_tiles)
        col_owner = divide(tile_col, tiles_dev, col_tiles)
        row_place, col_place = row_owner ^ rep, col_owner ^ row
        parity = col_place & 1
        group_row = ((row_place & 1) * 2 + parity) * half_rep + (row_place >> 1)
        row_block = group_row * tiles_dev + tile_row - row_owner * tiles_dev
        col_block = (col_place >> 1) * tiles_dev + tile_col - col_owner * tiles_dev
        return row_block * size, col_block * size

    def patch(row_start, col_start):
        rows = pl.ds(pl.multiple_of(row_start, size), size)
        return acc.at[rows, pl.ds(pl.multiple_of(col_start, size), size)]

    def add_group(first, largest):
        tiles = []
        for member in range(group_tiles):
            slot = first + member
            row_start, col_start = place(slot)
            row_start = jnp.where(slot < live, row_start, acc.shape[0] - size)
            col_start = jnp.where(slot < live, col_start, 0)
            tiles.append((row_start, col_start, held[slot].astype(f32).astype(bf16)))
        for row_start, col_start, tile in tiles:
            target = patch(row_start, col_start)
            total = target[...] + tile
            target[...] = total
            for part in range(0, size, 16):
                largest = jnp.maximum(largest, total[part:part + 16])
        return largest

    def add_chunk(index, largest):
        chunk_copy(index).wait()
        first = index * chunk
        groups = jnp.clip((live - first + group_tiles - 1) // group_tiles, 0, chunk // group_tiles)
        return lax.fori_loop(
            0, groups, lambda group, so_far: add_group(first + group * group_tiles, so_far), largest
        )

    largest = lax.fori_loop(0, slots // chunk, add_chunk, jnp.zeros((16, size), bf16))

    @pl.when(jnp.max(largest.astype(f32)) >= 256.0)
    def _():
        def redo(index, carry):
            row_start = index // (col_tiles // 2) * size
            col_start = index % (col_tiles // 2) * size
            exact[...] = jnp.zeros_like(exact)

            def add_tile(slot, inner):
                at_row, at_col = place(slot)

                @pl.when((at_row == row_start) & (at_col == col_start))
                def _():
                    exact[...] += held[slot]

                return inner

            lax.fori_loop(0, live, add_tile, 0)
            patch(row_start, col_start)[...] = exact[...].astype(f32).astype(bf16)
            return carry

        lax.fori_loop(0, row_tiles * col_tiles, redo, 0)


def dense_adjacency(tile_rows, tile_cols, live_tiles, counts, row_tiles, col_tiles, tiles_dev):
    slots, size, _ = counts.shape
    shape = ((2 * row_tiles + 1) * size, col_tiles // 2 * size)
    in_hbm = pl.BlockSpec(memory_space=pltpu.HBM)
    tile_rows, tile_cols, counts = [
        pltpu.with_memory_space_constraint(value, pltpu.HBM)
        for value in (tile_rows, tile_cols, counts)
    ]
    return pl.pallas_call(
        functools.partial(
            dense_kernel, row_tiles=row_tiles, col_tiles=col_tiles, tiles_dev=tiles_dev
        ),
        out_shape=pltpu.VMEM(shape, bf16),
        in_specs=[in_hbm, in_hbm, pl.BlockSpec(memory_space=pltpu.SMEM), in_hbm],
        out_specs=pl.BlockSpec(memory_space=pltpu.VMEM),
        scratch_shapes=[
            pltpu.VMEM(counts.shape, jnp.int32),
            pltpu.VMEM((size, size), jnp.int32),
            pltpu.SMEM(tile_rows.shape, jnp.int32),
            pltpu.SMEM(tile_cols.shape, jnp.int32),
            pltpu.SemaphoreType.DMA((slots // chunk_tiles,)),
            pltpu.SemaphoreType.DMA((2,)),
        ],
        compiler_params=pltpu.CompilerParams(
            vmem_limit_bytes=4 * counts.size + (3 << 20)
        ),
        cost_estimate=pl.CostEstimate(
            flops=shape[0] * shape[1], bytes_accessed=4 * counts.size, transcendentals=0
        ),
        name="dense_adjacency",
    )(tile_rows, tile_cols, live_tiles, counts)


def tile_sum(source, target_ids, source_ids, counts, live, out_rows, transpose):
    tile_size = counts.shape[-1]
    feature_width = source.shape[1]
    turn_count = (live + tiles_per_turn - 1) // tiles_per_turn
    pattern = "gji,gjf->gif" if transpose else "gij,gjf->gif"

    def one_turn(turn_index, running):
        first = turn_index * tiles_per_turn
        sources = lax.dynamic_slice_in_dim(source_ids, first, tiles_per_turn)
        targets = lax.dynamic_slice_in_dim(target_ids, first, tiles_per_turn)
        tiles_now = lax.dynamic_slice_in_dim(counts, first, tiles_per_turn, 0).astype(bf16)

        def one_piece(tile_index):
            return lax.dynamic_slice_in_dim(source, tile_index * tile_size, tile_size, 0)

        pieces = jax.vmap(one_piece)(sources)
        products = jnp.einsum(pattern, tiles_now, pieces, preferred_element_type=f32)
        active = first + jnp.arange(tiles_per_turn, dtype=jnp.int32) < live
        products = jnp.where(active[:, None, None], products, jnp.zeros_like(products))
        for member in range(tiles_per_turn):
            offset = targets[member] * tile_size
            current = lax.dynamic_slice_in_dim(running, offset, tile_size, 0)
            running = lax.dynamic_update_slice_in_dim(
                running, current + products[member], offset, 0
            )
        return running

    return lax.fori_loop(0, turn_count, one_turn, jnp.zeros((out_rows, feature_width), f32))


def after(value, *earlier):
    return lax.optimization_barrier((value, earlier))[0]


def gather_row(value, ready, others):
    size = lax.axis_size("row")
    pieces = {0: value}
    bit = size // 2
    while bit > 1:
        arrived = swap(value, "row", bit)
        pieces[bit] = after(arrived, *ready)
        ready = [*ready, arrived]
        bit //= 2
    singles = [pieces[place] for place in sorted(pieces) if place] + others
    bit = size // 2
    while bit > 1:
        for place in range(2 * bit, size, 2 * bit):
            pieces[place + bit] = swap(after(pieces[place], *singles), "row", bit)
        bit //= 2
    for place in range(0, size, 2):
        if place != 2:
            source = after(pieces[place], *singles) if place < size - 2 and place else pieces[place]
            pieces[place + 1] = swap(source, "row", 1)
    if size > 2:
        pieces[3] = swap(after(pieces[1], pieces[size - 2]), "row", 2)
    for place in range(5, size - 1, 2):
        pieces[place] = after(pieces[place], pieces[size - 2])
    return pieces


def pair_rows(bias_row):
    high = bias_row.astype(bf16).astype(f32)
    index = lax.broadcasted_iota(jnp.int32, (tail_rows, bias_row.shape[1]), 0)
    return jnp.where(index == 0, high, jnp.where(index == 1, bias_row - high, 0.0))


def message_kernel(*refs, width_rows):
    block_refs, (own_ref, moved_ref, out_ref) = refs[:-3], refs[-3:]
    nodes = out_ref.shape[0] - width_rows
    if nodes:
        total = block_refs[0][...]
        for ref in block_refs[1:]:
            total = total + ref[:nodes].astype(f32)
        out_ref[:nodes] = total.astype(out_ref.dtype)
    own = own_ref[own_ref.shape[0] - width_rows:].astype(f32)
    values = own + moved_ref[moved_ref.shape[0] - width_rows:].astype(f32)
    main = width_rows - tail_rows
    bias_row = values[main:main + 1] + values[main + 1:main + 2]
    out_ref[nodes:nodes + main] = values[:main].astype(out_ref.dtype)
    out_ref[nodes + main:] = pair_rows(bias_row).astype(out_ref.dtype)


def build_message(blocks, own, moved, width_rows, dtype=bf16):
    nodes = blocks[0].shape[0] if blocks else 0
    width = own.shape[1]
    whole = pl.BlockSpec(memory_space=pltpu.VMEM)
    return pl.pallas_call(
        functools.partial(message_kernel, width_rows=width_rows),
        out_shape=jax.ShapeDtypeStruct((nodes + width_rows, width), dtype),
        in_specs=[whole] * (len(blocks) + 2),
        out_specs=whole,
        compiler_params=pltpu.CompilerParams(vmem_limit_bytes=8 << 20),
        cost_estimate=pl.CostEstimate(
            flops=nodes * width, bytes_accessed=8 * nodes * width, transcendentals=0
        ),
        name="build_message",
    )(*blocks, own, moved)


def reduce_row(block, own, start_payload):
    def message(value, *earlier):
        return after(value.astype(bf16), *earlier)

    nodes = own.shape[0]
    payload, begun = start_payload(own)
    width_rows = payload.shape[0]
    far7 = message(block(7, begun))
    moved7 = swap(far7, "row", 2)
    rows_moved = swap(payload, "row", 4)
    far3 = message(block(3, far7))
    moved3 = swap(far3, "row", 1)
    near6 = block(6, far3)
    far5 = block(5, near6)
    sent6 = build_message([near6], payload, rows_moved, width_rows)
    moved6 = swap(sent6, "row", 2)
    moved5 = swap(message(far5 + moved7.astype(f32), moved3), "row", 1)
    near4 = block(4, sent6)
    near4 = message(near4 + moved5.astype(f32) + moved6[:nodes].astype(f32))
    moved4 = swap(near4, "row", 4)
    near2 = message(block(2, sent6) + moved3.astype(f32))
    moved2 = swap(near2, "row", 2)
    sent1 = build_message([block(1, near4)], sent6, moved6, width_rows)
    moved1 = swap(sent1, "row", 1)
    payload = build_message([], sent1, moved1, width_rows)
    total = block(0, near2) + own.astype(f32) + moved2.astype(f32) + moved1[:nodes].astype(f32)
    return total + moved4.astype(f32), payload


def reduce_row_plainly(block, own, start_payload):
    size = lax.axis_size("row")
    sums = {place: block(place) for place in range(size)}
    sums[0] = sums[0] + own.astype(f32)
    payload, _ = start_payload(sums[size - 1].astype(bf16))
    bit = 1
    while bit < size:
        for place in sorted(sums, reverse=True):
            if place & bit:
                moved = swap(sums.pop(place).astype(bf16), "row", bit)
                sums[place - bit] = sums[place - bit] + moved.astype(f32)
        payload = build_message([], payload, swap(payload, "row", bit), payload.shape[0])
        bit *= 2
    return sums[0], payload


def reduce_rep(sums):
    sums = dict(sums)
    bit = 1
    while bit < lax.axis_size("rep"):
        for place in sorted(sums, reverse=True):
            if place & bit:
                moved = swap(sums.pop(place).astype(bf16), "rep", bit)
                sums[place - bit] = sums[place - bit] + moved.astype(f32)
        bit *= 2
    return sums[0]


def weight_kernel(*refs, parts, distances):
    summed_refs, scaled_refs, grad_refs = refs[:parts], refs[parts:2 * parts], refs[2 * parts:3 * parts]
    out_ref, whole = refs[-2:]
    rows = out_ref.shape[1] - tail_rows
    rep = lax.axis_index("rep")
    weight_part, bias_row = 0.0, 0.0
    for summed_ref, scaled_ref, grad_ref in zip(summed_refs, scaled_refs, grad_refs):
        weight_part += lax.dot_general(
            summed_ref[...], scaled_ref[...].astype(f32), (((0,), (0,)), ((), ())),
            precision=lax.Precision.HIGHEST, preferred_element_type=f32,
        )
        bias_row += jnp.sum(grad_ref[...], axis=0, keepdims=True)
    whole[...] = weight_part
    for index, distance in enumerate(distances):
        start = pl.multiple_of((rep ^ distance) * rows, rows)
        out_ref[index, :rows] = whole[pl.ds(start, rows)]
        out_ref[index, rows:] = pair_rows(bias_row)


def weight_blocks(summed, scaled, grads, earlier, n_rep, distances):
    nodes, width = summed[0].shape
    parts = len(summed)
    whole = pl.BlockSpec(memory_space=pltpu.VMEM)
    return pl.pallas_call(
        functools.partial(weight_kernel, parts=parts, distances=distances),
        out_shape=jax.ShapeDtypeStruct((len(distances), width // n_rep + tail_rows, width), f32),
        in_specs=[whole] * (3 * parts) + [pl.BlockSpec(memory_space=pl.ANY)],
        out_specs=whole,
        scratch_shapes=[pltpu.VMEM((width, width), f32)],
        compiler_params=pltpu.CompilerParams(vmem_limit_bytes=8 << 20),
        cost_estimate=pl.CostEstimate(
            flops=12 * parts * nodes * width * width,
            bytes_accessed=16 * parts * nodes * width,
            transcendentals=0,
        ),
        name="weight_blocks",
    )(*summed, *scaled, *grads, earlier)


def join_kernel(*refs):
    part_refs, (out_ref, bias_ref) = refs[:-2], refs[-2:]
    rows = out_ref.shape[0] // len(part_refs)
    rep = lax.axis_index("rep")
    bias_row = jnp.zeros_like(bias_ref)
    for distance, ref in enumerate(part_refs):
        values = ref[...].astype(f32)
        out_ref[pl.ds(pl.multiple_of((rep ^ distance) * rows, rows), rows)] = values[:rows]
        bias_row = jnp.where(rep == distance, values[rows:rows + 1] + values[rows + 1:rows + 2], bias_row)
    bias_ref[...] = bias_row


def weight_part(blocks, distances):
    total = blocks[0]
    for index, distance in enumerate(distances):
        if distance:
            total = build_message([], total, swap(blocks[index], "rep", distance), total.shape[0], f32)
    return total


def weight_join(total, n_rep, earlier):
    rows, width = total.shape
    rows -= tail_rows
    parts = [total]
    parts += [after(swap(total, "rep", distance), earlier) for distance in range(1, n_rep)]
    whole = pl.BlockSpec(memory_space=pltpu.VMEM)
    grad_weight, grad_bias = pl.pallas_call(
        join_kernel,
        out_shape=[
            jax.ShapeDtypeStruct((n_rep * rows, width), f32),
            jax.ShapeDtypeStruct((1, width), f32),
        ],
        in_specs=[whole] * n_rep,
        out_specs=[whole] * 2,
        compiler_params=pltpu.CompilerParams(vmem_limit_bytes=4 << 20),
        cost_estimate=pl.CostEstimate(
            flops=n_rep * rows * width, bytes_accessed=8 * n_rep * rows * width, transcendentals=0
        ),
        name="join_blocks",
    )(*parts)
    return grad_weight, grad_bias.reshape(width)


def body(feats, weight, bias, degree, tile_rows, tile_cols, tile_counts, live_tiles, cotangent):
    node_dev, width = feats.shape
    n_row, n_rep = lax.axis_size("row"), lax.axis_size("rep")
    row, rep = lax.axis_index("row"), lax.axis_index("rep")
    counts = tile_counts[0, 0]
    size = counts.shape[-1]
    tiles_dev = node_dev // size
    row_tiles, col_tiles = tiles_dev * n_rep, tiles_dev * n_row
    half_row, half_rep = n_row // 2, n_rep // 2

    paired = n_rep == 4
    places = (0, 2) if paired else (0,)

    inv_row = lax.rsqrt(degree.astype(f32))
    inv = {
        place: lax.dynamic_slice_in_dim(inv_row, (rep ^ place) * node_dev, node_dev)[:, None]
        for place in places
    }
    inv_own = inv[0]
    cotangents = {0: cotangent}
    if paired:
        cotangents[2] = swap(cotangent, "rep", 2)

    dense = row_tiles * col_tiles <= dense_limit
    if dense:
        adjacency = dense_adjacency(
            after(tile_rows, *inv.values()), tile_cols, live_tiles, counts,
            row_tiles, col_tiles, tiles_dev,
        )
    else:
        live = live_tiles[0, 0]
        row_ids = ((tile_rows[0, 0] // tiles_dev) ^ rep) * tiles_dev + tile_rows[0, 0] % tiles_dev
        col_place = (tile_cols[0, 0] // tiles_dev) ^ row
        col_place = col_place // 2 + col_place % 2 * half_row
        col_ids = col_place * tiles_dev + tile_cols[0, 0] % tiles_dev

    scaled_x = (inv_own * feats.astype(f32)).astype(bf16)

    pieces = gather_row(scaled_x, [adjacency] if dense else (), [cotangents[2]] if paired else [])
    even = jnp.concatenate([pieces[place] for place in range(0, n_row, 2)])
    odd = jnp.concatenate([pieces[place] for place in range(1, n_row - 1, 2)])

    if dense:
        def block(place, parity, count=1):
            first = ((place % 2 * 2 + parity) * half_rep + place // 2) * node_dev
            return adjacency[first:first + count * node_dev]

        def aggregate(place):
            most = (half_row - 1) * node_dev
            even_cols, odd_cols = block(place, 0, half_rep), block(place, 1, half_rep)
            before = jnp.dot(even_cols, even, preferred_element_type=f32)
            before = before + jnp.dot(odd_cols[:, :most], odd, preferred_element_type=f32)
            return before + jnp.dot(odd_cols[:, most:], pieces[n_row - 1], preferred_element_type=f32)

        near_sum, far_sum = aggregate(0), aggregate(1)
    else:
        sums = tile_sum(
            jnp.concatenate([even, odd, pieces[n_row - 1]]), row_ids, col_ids, counts, live,
            row_tiles * size, False,
        ).reshape(half_rep, 2, node_dev, width)
        near_sum, far_sum = sums[:, 0].reshape(-1, width), sums[:, 1].reshape(-1, width)
    near_sum = near_sum + swap(far_sum.astype(bf16), "rep", 1).astype(f32)
    near_sum = near_sum + jnp.pad(
        scaled_x.astype(f32), ((0, near_sum.shape[0] - node_dev), (0, 0))
    )
    if paired:
        other = swap(near_sum.astype(bf16), "rep", 2)
        summed = {
            0: near_sum[:node_dev] + other[node_dev:].astype(f32),
            2: near_sum[node_dev:] + other[:node_dev].astype(f32),
        }
    else:
        near_sum = near_sum.reshape(half_rep, node_dev, width)
        summed = {0: reduce_rep({2 * place: near_sum[place] for place in range(half_rep)})}

    def activate(place):
        z = inv[place] * jnp.dot(
            summed[place], weight.astype(f32),
            precision=lax.Precision.HIGHEST, preferred_element_type=f32,
        ) + bias
        sigmoid_z = jax.nn.sigmoid(z)
        grad_z = cotangents[place].astype(f32) * sigmoid_z * (1.0 + z * (1.0 - sigmoid_z))
        return (z * sigmoid_z).astype(bf16), grad_z, (inv[place] * grad_z).astype(bf16)

    outputs, grads, received = {}, {}, {}
    for place in places:
        outputs[place], grads[place], received[place] = activate(place)
    output, scaled_r = outputs[0], received[0]
    for bit in reversed(range(n_rep.bit_length() - 1)):
        for place in sorted(received):
            if place + (1 << bit) < n_rep and not place % (2 << bit) and place + (1 << bit) not in received:
                received[place + (1 << bit)] = swap(received[place], "rep", 1 << bit)

    def transposed(matrix, value):
        return lax.dot_general(matrix, value, (((0,), (0,)), ((), ())), preferred_element_type=f32)

    if dense:
        begun = {}
        late = [place for place in range(1, n_rep, 2)]

        def back_block(index, *earlier):
            parity = index % 2
            if parity not in begun:
                begun[parity] = 0.0
                for place in range(0, n_rep, 2):
                    value = after(received[place], *earlier)
                    begun[parity] = begun[parity] + transposed(block(place, parity), value)
            part = slice(index // 2 * node_dev, (index // 2 + 1) * node_dev)
            total = begun[parity][part]
            for place in late:
                value = after(received[place], received[late[-1]], *earlier)
                total = total + transposed(block(place, parity)[:, part], value)
            return total
    else:
        backward = tile_sum(
            jnp.concatenate([received[place] for place in range(n_rep)]),
            col_ids, row_ids, counts, live, col_tiles * size, True,
        ).reshape(n_row, node_dev, width)

        def back_block(index, *earlier):
            return backward[index // 2 + index % 2 * half_row]

    def start_payload(earlier):
        distances = (0, 1) if paired else tuple(range(n_rep))
        blocks = weight_blocks(
            [summed[place] for place in places], [received[place] for place in places],
            [grads[place] for place in places], earlier, n_rep, distances,
        )
        return weight_part(blocks, distances), blocks

    reduce_over_row = reduce_row if n_row == 8 else reduce_row_plainly
    grad_q, weight_total = reduce_over_row(back_block, scaled_r, start_payload)
    v_half = after((inv_own * grad_q).astype(bf16))
    grad_feats = jnp.dot(v_half, weight.T, preferred_element_type=f32).astype(bf16)
    grad_weight, grad_bias = weight_join(weight_total, n_rep, grad_feats)
    return (output, grad_feats, grad_weight, grad_bias)


def solution(mesh):
    return jax.shard_map(
        body,
        mesh=mesh,
        in_specs=(
            P(("row", "rep"), None),
            P(),
            P(),
            P("row"),
            P("row", "rep", None),
            P("row", "rep", None),
            P("row", "rep", None, None, None),
            P("row", "rep"),
            P(("row", "rep"), None),
        ),
        out_specs=(P(("row", "rep"), None), P(("row", "rep"), None), P(), P()),
        check_vma=False,
    )
```

```python
import functools

import jax
import jax.numpy as jnp
from jax import lax
from jax.experimental import pallas as pl
from jax.experimental.pallas import tpu as pltpu
from jax.sharding import PartitionSpec as P

tiles_per_turn = 8
chunk_tiles = 16
group_tiles = 4
dense_limit = 512
tail_rows = 16
f32 = jnp.float32
bf16 = jnp.bfloat16


def swap(value, axis, distance):
    size = lax.axis_size(axis)
    return lax.ppermute(value, axis, [(i, i ^ distance) for i in range(size)])


def divide(value, divisor, limit):
    factor = (1 << 16) // divisor + 1
    assert all(n * factor >> 16 == n // divisor for n in range(limit))
    return (value * factor) >> 16


def dense_kernel(
    rows_hbm, cols_hbm, live_ref, counts_ref, acc, held, exact, rows_ref, cols_ref,
    in_sems, small_sems, *, row_tiles, col_tiles, tiles_dev
):
    slots, size, _ = held.shape
    chunk = slots // in_sems.shape[0]
    half_cols = acc.shape[1]
    half_rep = row_tiles // tiles_dev // 2
    row, rep = lax.axis_index("row"), lax.axis_index("rep")

    small_copies = [
        pltpu.make_async_copy(source, target, small_sems.at[index])
        for index, (source, target) in enumerate(
            [(rows_hbm, rows_ref), (cols_hbm, cols_ref)]
        )
    ]
    for copy in small_copies:
        copy.start()

    def chunk_copy(index):
        part = pl.ds(index * chunk, chunk)
        return pltpu.make_async_copy(counts_ref.at[part], held.at[part], in_sems.at[index])

    def start_copy(index, carry):
        chunk_copy(index).start()
        return carry

    lax.fori_loop(0, slots // chunk, start_copy, 0)

    def clear(index, carry):
        part = pl.ds(pl.multiple_of(index * size, size), size)
        acc[part] = jnp.zeros((size, half_cols), bf16)
        return carry

    lax.fori_loop(0, acc.shape[0] // size, clear, 0)
    for copy in small_copies:
        copy.wait()
    live = live_ref[0, 0]

    def place(slot):
        tile_row, tile_col = rows_ref[0, 0, slot], cols_ref[0, 0, slot]
        row_owner = divide(tile_row, tiles_dev, row_tiles)
        col_owner = divide(tile_col, tiles_dev, col_tiles)
        row_place, col_place = row_owner ^ rep, col_owner ^ row
        parity = col_place & 1
        group_row = ((row_place & 1) * 2 + parity) * half_rep + (row_place >> 1)
        row_block = group_row * tiles_dev + tile_row - row_owner * tiles_dev
        col_block = (col_place >> 1) * tiles_dev + tile_col - col_owner * tiles_dev
        return row_block * size, col_block * size

    def patch(row_start, col_start):
        rows = pl.ds(pl.multiple_of(row_start, size), size)
        return acc.at[rows, pl.ds(pl.multiple_of(col_start, size), size)]

    def add_group(first, largest):
        tiles = []
        for member in range(group_tiles):
            slot = first + member
            row_start, col_start = place(slot)
            row_start = jnp.where(slot < live, row_start, acc.shape[0] - size)
            col_start = jnp.where(slot < live, col_start, 0)
            tiles.append((row_start, col_start, held[slot].astype(f32).astype(bf16)))
        for row_start, col_start, tile in tiles:
            target = patch(row_start, col_start)
            total = target[...] + tile
            target[...] = total
            for part in range(0, size, 16):
                largest = jnp.maximum(largest, total[part:part + 16])
        return largest

    def add_chunk(index, largest):
        chunk_copy(index).wait()
        first = index * chunk
        groups = jnp.clip((live - first + group_tiles - 1) // group_tiles, 0, chunk // group_tiles)
        return lax.fori_loop(
            0, groups, lambda group, so_far: add_group(first + group * group_tiles, so_far), largest
        )

    largest = lax.fori_loop(0, slots // chunk, add_chunk, jnp.zeros((16, size), bf16))

    @pl.when(jnp.max(largest.astype(f32)) >= 256.0)
    def _():
        def redo(index, carry):
            row_start = index // (col_tiles // 2) * size
            col_start = index % (col_tiles // 2) * size
            exact[...] = jnp.zeros_like(exact)

            def add_tile(slot, inner):
                at_row, at_col = place(slot)

                @pl.when((at_row == row_start) & (at_col == col_start))
                def _():
                    exact[...] += held[slot]

                return inner

            lax.fori_loop(0, live, add_tile, 0)
            patch(row_start, col_start)[...] = exact[...].astype(f32).astype(bf16)
            return carry

        lax.fori_loop(0, row_tiles * col_tiles, redo, 0)


def dense_adjacency(tile_rows, tile_cols, live_tiles, counts, row_tiles, col_tiles, tiles_dev):
    slots, size, _ = counts.shape
    shape = ((2 * row_tiles + 1) * size, col_tiles // 2 * size)
    in_hbm = pl.BlockSpec(memory_space=pltpu.HBM)
    tile_rows, tile_cols, counts = [
        pltpu.with_memory_space_constraint(value, pltpu.HBM)
        for value in (tile_rows, tile_cols, counts)
    ]
    return pl.pallas_call(
        functools.partial(
            dense_kernel, row_tiles=row_tiles, col_tiles=col_tiles, tiles_dev=tiles_dev
        ),
        out_shape=pltpu.VMEM(shape, bf16),
        in_specs=[in_hbm, in_hbm, pl.BlockSpec(memory_space=pltpu.SMEM), in_hbm],
        out_specs=pl.BlockSpec(memory_space=pltpu.VMEM),
        scratch_shapes=[
            pltpu.VMEM(counts.shape, jnp.int32),
            pltpu.VMEM((size, size), jnp.int32),
            pltpu.SMEM(tile_rows.shape, jnp.int32),
            pltpu.SMEM(tile_cols.shape, jnp.int32),
            pltpu.SemaphoreType.DMA((slots // chunk_tiles,)),
            pltpu.SemaphoreType.DMA((2,)),
        ],
        compiler_params=pltpu.CompilerParams(
            vmem_limit_bytes=4 * counts.size + (3 << 20)
        ),
        cost_estimate=pl.CostEstimate(
            flops=shape[0] * shape[1], bytes_accessed=4 * counts.size, transcendentals=0
        ),
        name="dense_adjacency",
    )(tile_rows, tile_cols, live_tiles, counts)


def tile_sum(source, target_ids, source_ids, counts, live, out_rows, transpose):
    tile_size = counts.shape[-1]
    feature_width = source.shape[1]
    turn_count = (live + tiles_per_turn - 1) // tiles_per_turn
    pattern = "gji,gjf->gif" if transpose else "gij,gjf->gif"

    def one_turn(turn_index, running):
        first = turn_index * tiles_per_turn
        sources = lax.dynamic_slice_in_dim(source_ids, first, tiles_per_turn)
        targets = lax.dynamic_slice_in_dim(target_ids, first, tiles_per_turn)
        tiles_now = lax.dynamic_slice_in_dim(counts, first, tiles_per_turn, 0).astype(bf16)

        def one_piece(tile_index):
            return lax.dynamic_slice_in_dim(source, tile_index * tile_size, tile_size, 0)

        pieces = jax.vmap(one_piece)(sources)
        products = jnp.einsum(pattern, tiles_now, pieces, preferred_element_type=f32)
        active = first + jnp.arange(tiles_per_turn, dtype=jnp.int32) < live
        products = jnp.where(active[:, None, None], products, jnp.zeros_like(products))
        for member in range(tiles_per_turn):
            offset = targets[member] * tile_size
            current = lax.dynamic_slice_in_dim(running, offset, tile_size, 0)
            running = lax.dynamic_update_slice_in_dim(
                running, current + products[member], offset, 0
            )
        return running

    return lax.fori_loop(0, turn_count, one_turn, jnp.zeros((out_rows, feature_width), f32))


def after(value, *earlier):
    return lax.optimization_barrier((value, earlier))[0]


def gather_row(value, ready, others):
    size = lax.axis_size("row")
    pieces = {0: value}
    bit = size // 2
    while bit > 1:
        arrived = swap(value, "row", bit)
        pieces[bit] = after(arrived, *ready)
        ready = [*ready, arrived]
        bit //= 2
    singles = [pieces[place] for place in sorted(pieces) if place] + others
    bit = size // 2
    while bit > 1:
        for place in range(2 * bit, size, 2 * bit):
            pieces[place + bit] = swap(after(pieces[place], *singles), "row", bit)
        bit //= 2
    for place in range(0, size, 2):
        if place != 2:
            source = after(pieces[place], *singles) if place < size - 2 and place else pieces[place]
            pieces[place + 1] = swap(source, "row", 1)
    if size > 2:
        pieces[3] = swap(after(pieces[1], pieces[size - 2]), "row", 2)
    for place in range(5, size - 1, 2):
        pieces[place] = after(pieces[place], pieces[size - 2])
    return pieces


def pair_rows(bias_row):
    high = bias_row.astype(bf16).astype(f32)
    index = lax.broadcasted_iota(jnp.int32, (tail_rows, bias_row.shape[1]), 0)
    return jnp.where(index == 0, high, jnp.where(index == 1, bias_row - high, 0.0))


def message_kernel(*refs, width_rows):
    block_refs, (own_ref, moved_ref, out_ref) = refs[:-3], refs[-3:]
    nodes = out_ref.shape[0] - width_rows
    if nodes:
        total = block_refs[0][...]
        for ref in block_refs[1:]:
            total = total + ref[:nodes].astype(f32)
        out_ref[:nodes] = total.astype(out_ref.dtype)
    own = own_ref[own_ref.shape[0] - width_rows:].astype(f32)
    values = own + moved_ref[moved_ref.shape[0] - width_rows:].astype(f32)
    main = width_rows - tail_rows
    bias_row = values[main:main + 1] + values[main + 1:main + 2]
    out_ref[nodes:nodes + main] = values[:main].astype(out_ref.dtype)
    out_ref[nodes + main:] = pair_rows(bias_row).astype(out_ref.dtype)


def build_message(blocks, own, moved, width_rows, dtype=bf16):
    nodes = blocks[0].shape[0] if blocks else 0
    width = own.shape[1]
    whole = pl.BlockSpec(memory_space=pltpu.VMEM)
    return pl.pallas_call(
        functools.partial(message_kernel, width_rows=width_rows),
        out_shape=jax.ShapeDtypeStruct((nodes + width_rows, width), dtype),
        in_specs=[whole] * (len(blocks) + 2),
        out_specs=whole,
        compiler_params=pltpu.CompilerParams(vmem_limit_bytes=8 << 20),
        cost_estimate=pl.CostEstimate(
            flops=nodes * width, bytes_accessed=8 * nodes * width, transcendentals=0
        ),
        name="build_message",
    )(*blocks, own, moved)


def reduce_row(block, own, start_payload):
    def message(value, *earlier):
        return after(value.astype(bf16), *earlier)

    nodes = own.shape[0]
    payload, begun = start_payload(own)
    width_rows = payload.shape[0]
    far7 = message(block(7, begun))
    moved7 = swap(far7, "row", 2)
    rows_moved = swap(payload, "row", 4)
    far3 = message(block(3, far7))
    moved3 = swap(far3, "row", 1)
    near6 = block(6, far3)
    far5 = block(5, near6)
    sent6 = build_message([near6], payload, rows_moved, width_rows)
    moved6 = swap(sent6, "row", 2)
    moved5 = swap(message(far5 + moved7.astype(f32), moved3), "row", 1)
    near4 = block(4, sent6)
    near4 = message(near4 + moved5.astype(f32) + moved6[:nodes].astype(f32))
    moved4 = swap(near4, "row", 4)
    far1 = block(1, sent6)
    near2 = message(block(2, far1) + moved3.astype(f32))
    moved2 = swap(near2, "row", 2)
    sent1 = build_message([after(far1, near4)], sent6, moved6, width_rows)
    moved1 = swap(sent1, "row", 1)
    payload = build_message([], sent1, moved1, width_rows)
    total = block(0, near2) + own.astype(f32) + moved2.astype(f32) + moved1[:nodes].astype(f32)
    return total + moved4.astype(f32), payload


def reduce_row_plainly(block, own, start_payload):
    size = lax.axis_size("row")
    sums = {place: block(place) for place in range(size)}
    sums[0] = sums[0] + own.astype(f32)
    payload, _ = start_payload(sums[size - 1].astype(bf16))
    bit = 1
    while bit < size:
        for place in sorted(sums, reverse=True):
            if place & bit:
                moved = swap(sums.pop(place).astype(bf16), "row", bit)
                sums[place - bit] = sums[place - bit] + moved.astype(f32)
        payload = build_message([], payload, swap(payload, "row", bit), payload.shape[0])
        bit *= 2
    return sums[0], payload


def reduce_rep(sums):
    sums = dict(sums)
    bit = 1
    while bit < lax.axis_size("rep"):
        for place in sorted(sums, reverse=True):
            if place & bit:
                moved = swap(sums.pop(place).astype(bf16), "rep", bit)
                sums[place - bit] = sums[place - bit] + moved.astype(f32)
        bit *= 2
    return sums[0]


def weight_kernel(*refs, parts, distances):
    summed_refs, scaled_refs, grad_refs = refs[:parts], refs[parts:2 * parts], refs[2 * parts:3 * parts]
    out_ref, whole = refs[-2:]
    rows = out_ref.shape[1] - tail_rows
    rep = lax.axis_index("rep")
    weight_part, bias_row = 0.0, 0.0
    for summed_ref, scaled_ref, grad_ref in zip(summed_refs, scaled_refs, grad_refs):
        weight_part += lax.dot_general(
            summed_ref[...], scaled_ref[...].astype(f32), (((0,), (0,)), ((), ())),
            precision=lax.Precision.HIGHEST, preferred_element_type=f32,
        )
        bias_row += jnp.sum(grad_ref[...], axis=0, keepdims=True)
    whole[...] = weight_part
    for index, distance in enumerate(distances):
        start = pl.multiple_of((rep ^ distance) * rows, rows)
        out_ref[index, :rows] = whole[pl.ds(start, rows)]
        out_ref[index, rows:] = pair_rows(bias_row)


def weight_blocks(summed, scaled, grads, earlier, n_rep, distances):
    nodes, width = summed[0].shape
    parts = len(summed)
    whole = pl.BlockSpec(memory_space=pltpu.VMEM)
    return pl.pallas_call(
        functools.partial(weight_kernel, parts=parts, distances=distances),
        out_shape=jax.ShapeDtypeStruct((len(distances), width // n_rep + tail_rows, width), f32),
        in_specs=[whole] * (3 * parts) + [pl.BlockSpec(memory_space=pl.ANY)],
        out_specs=whole,
        scratch_shapes=[pltpu.VMEM((width, width), f32)],
        compiler_params=pltpu.CompilerParams(vmem_limit_bytes=8 << 20),
        cost_estimate=pl.CostEstimate(
            flops=12 * parts * nodes * width * width,
            bytes_accessed=16 * parts * nodes * width,
            transcendentals=0,
        ),
        name="weight_blocks",
    )(*summed, *scaled, *grads, earlier)


def join_kernel(*refs):
    part_refs, (out_ref, bias_ref) = refs[:-2], refs[-2:]
    rows = out_ref.shape[0] // len(part_refs)
    rep = lax.axis_index("rep")
    bias_row = jnp.zeros_like(bias_ref)
    for distance, ref in enumerate(part_refs):
        values = ref[...].astype(f32)
        out_ref[pl.ds(pl.multiple_of((rep ^ distance) * rows, rows), rows)] = values[:rows]
        bias_row = jnp.where(rep == distance, values[rows:rows + 1] + values[rows + 1:rows + 2], bias_row)
    bias_ref[...] = bias_row


def weight_part(blocks, distances):
    total = blocks[0]
    for index, distance in enumerate(distances):
        if distance:
            total = build_message([], total, swap(blocks[index], "rep", distance), total.shape[0], f32)
    return total


def weight_join(total, n_rep, earlier):
    rows, width = total.shape
    rows -= tail_rows
    parts = [total]
    parts += [after(swap(total, "rep", distance), earlier) for distance in range(1, n_rep)]
    whole = pl.BlockSpec(memory_space=pltpu.VMEM)
    grad_weight, grad_bias = pl.pallas_call(
        join_kernel,
        out_shape=[
            jax.ShapeDtypeStruct((n_rep * rows, width), f32),
            jax.ShapeDtypeStruct((1, width), f32),
        ],
        in_specs=[whole] * n_rep,
        out_specs=[whole] * 2,
        compiler_params=pltpu.CompilerParams(vmem_limit_bytes=4 << 20),
        cost_estimate=pl.CostEstimate(
            flops=n_rep * rows * width, bytes_accessed=8 * n_rep * rows * width, transcendentals=0
        ),
        name="join_blocks",
    )(*parts)
    return grad_weight, grad_bias.reshape(width)


def body(feats, weight, bias, degree, tile_rows, tile_cols, tile_counts, live_tiles, cotangent):
    node_dev, width = feats.shape
    n_row, n_rep = lax.axis_size("row"), lax.axis_size("rep")
    row, rep = lax.axis_index("row"), lax.axis_index("rep")
    counts = tile_counts[0, 0]
    size = counts.shape[-1]
    tiles_dev = node_dev // size
    row_tiles, col_tiles = tiles_dev * n_rep, tiles_dev * n_row
    half_row, half_rep = n_row // 2, n_rep // 2

    paired = n_rep == 4
    places = (0, 2) if paired else (0,)

    inv_row = lax.rsqrt(degree.astype(f32))
    inv = {
        place: lax.dynamic_slice_in_dim(inv_row, (rep ^ place) * node_dev, node_dev)[:, None]
        for place in places
    }
    inv_own = inv[0]
    cotangents = {0: cotangent}
    if paired:
        cotangents[2] = swap(cotangent, "rep", 2)

    dense = row_tiles * col_tiles <= dense_limit
    if dense:
        adjacency = dense_adjacency(
            after(tile_rows, *inv.values()), tile_cols, live_tiles, counts,
            row_tiles, col_tiles, tiles_dev,
        )
    else:
        live = live_tiles[0, 0]
        row_ids = ((tile_rows[0, 0] // tiles_dev) ^ rep) * tiles_dev + tile_rows[0, 0] % tiles_dev
        col_place = (tile_cols[0, 0] // tiles_dev) ^ row
        col_place = col_place // 2 + col_place % 2 * half_row
        col_ids = col_place * tiles_dev + tile_cols[0, 0] % tiles_dev

    scaled_x = (inv_own * feats.astype(f32)).astype(bf16)

    pieces = gather_row(scaled_x, [adjacency] if dense else (), [cotangents[2]] if paired else [])
    even = jnp.concatenate([pieces[place] for place in range(0, n_row, 2)])
    odd = jnp.concatenate([pieces[place] for place in range(1, n_row - 1, 2)])

    if dense:
        def block(place, parity, count=1):
            first = ((place % 2 * 2 + parity) * half_rep + place // 2) * node_dev
            return adjacency[first:first + count * node_dev]

        def aggregate(place):
            most = (half_row - 1) * node_dev
            even_cols, odd_cols = block(place, 0, half_rep), block(place, 1, half_rep)
            before = jnp.dot(even_cols, even, preferred_element_type=f32)
            before = before + jnp.dot(odd_cols[:, :most], odd, preferred_element_type=f32)
            return before + jnp.dot(odd_cols[:, most:], pieces[n_row - 1], preferred_element_type=f32)

        near_sum, far_sum = aggregate(0), aggregate(1)
    else:
        sums = tile_sum(
            jnp.concatenate([even, odd, pieces[n_row - 1]]), row_ids, col_ids, counts, live,
            row_tiles * size, False,
        ).reshape(half_rep, 2, node_dev, width)
        near_sum, far_sum = sums[:, 0].reshape(-1, width), sums[:, 1].reshape(-1, width)
    near_sum = near_sum + swap(far_sum.astype(bf16), "rep", 1).astype(f32)
    near_sum = near_sum + jnp.pad(
        scaled_x.astype(f32), ((0, near_sum.shape[0] - node_dev), (0, 0))
    )
    if paired:
        other = swap(near_sum.astype(bf16), "rep", 2)
        summed = {
            0: near_sum[:node_dev] + other[node_dev:].astype(f32),
            2: near_sum[node_dev:] + other[:node_dev].astype(f32),
        }
    else:
        near_sum = near_sum.reshape(half_rep, node_dev, width)
        summed = {0: reduce_rep({2 * place: near_sum[place] for place in range(half_rep)})}

    def activate(place):
        z = inv[place] * jnp.dot(
            summed[place], weight.astype(f32),
            precision=lax.Precision.HIGHEST, preferred_element_type=f32,
        ) + bias
        sigmoid_z = jax.nn.sigmoid(z)
        grad_z = cotangents[place].astype(f32) * sigmoid_z * (1.0 + z * (1.0 - sigmoid_z))
        return (z * sigmoid_z).astype(bf16), grad_z, (inv[place] * grad_z).astype(bf16)

    outputs, grads, received = {}, {}, {}
    for place in places:
        outputs[place], grads[place], received[place] = activate(place)
    output, scaled_r = outputs[0], received[0]
    for bit in reversed(range(n_rep.bit_length() - 1)):
        for place in sorted(received):
            if place + (1 << bit) < n_rep and not place % (2 << bit) and place + (1 << bit) not in received:
                received[place + (1 << bit)] = swap(received[place], "rep", 1 << bit)

    def transposed(matrix, value):
        return lax.dot_general(matrix, value, (((0,), (0,)), ((), ())), preferred_element_type=f32)

    if dense:
        begun = {}
        late = [place for place in range(1, n_rep, 2)]

        def back_block(index, *earlier):
            parity = index % 2
            if parity not in begun:
                begun[parity] = 0.0
                for place in range(0, n_rep, 2):
                    value = after(received[place], *earlier)
                    begun[parity] = begun[parity] + transposed(block(place, parity), value)
            part = slice(index // 2 * node_dev, (index // 2 + 1) * node_dev)
            total = begun[parity][part]
            for place in late:
                value = after(received[place], received[late[-1]], *earlier)
                total = total + transposed(block(place, parity)[:, part], value)
            return total
    else:
        backward = tile_sum(
            jnp.concatenate([received[place] for place in range(n_rep)]),
            col_ids, row_ids, counts, live, col_tiles * size, True,
        ).reshape(n_row, node_dev, width)

        def back_block(index, *earlier):
            return backward[index // 2 + index % 2 * half_row]

    def start_payload(earlier):
        distances = (0, 1) if paired else tuple(range(n_rep))
        blocks = weight_blocks(
            [summed[place] for place in places], [received[place] for place in places],
            [grads[place] for place in places], earlier, n_rep, distances,
        )
        return weight_part(blocks, distances), blocks

    reduce_over_row = reduce_row if n_row == 8 else reduce_row_plainly
    grad_q, weight_total = reduce_over_row(back_block, scaled_r, start_payload)
    v_half = after((inv_own * grad_q).astype(bf16))
    grad_feats = jnp.dot(v_half, weight.T, preferred_element_type=f32).astype(bf16)
    grad_weight, grad_bias = weight_join(weight_total, n_rep, grad_feats)
    return (output, grad_feats, grad_weight, grad_bias)


def solution(mesh):
    return jax.shard_map(
        body,
        mesh=mesh,
        in_specs=(
            P(("row", "rep"), None),
            P(),
            P(),
            P("row"),
            P("row", "rep", None),
            P("row", "rep", None),
            P("row", "rep", None, None, None),
            P("row", "rep"),
            P(("row", "rep"), None),
        ),
        out_specs=(P(("row", "rep"), None), P(("row", "rep"), None), P(), P()),
        check_vma=False,
    )
```
